32 devices in a mesh: sx: 8 (over y, x, core), sy: 4 (over z).
Axes of the slice: x: 2, y: 2, z: 4, core: 2. Of those that a mesh axis runs over, the one named last changes fastest.
Arguments:
- schur_diag: bfloat16 [4, 8, 4, 512, 512], P('sy', 'sx'), may hold values from 0 to 17, as said below
- coupling: bfloat16 [4, 8, 3, 512, 512], P('sy', 'sx'), may hold values from 0 to 4
- right_side: float32 [4, 8, 4, 512], P('sy', 'sx'), may hold values from -12 to 12
- face_link: int32 [4, 8, 4], P('sy', 'sx'), may hold values from 0 to 1, as said below
- face_start: int32 [4, 8, 4], P('sy', 'sx'), may hold values from 0 to 1536, as said below
Outputs:
- solution_field: float32 [4, 8, 4, 512], P('sy', 'sx')
- residual: float32 [4, 8, 4, 512], P('sy', 'sx')
The draws below stay inside these ranges and needn't reach their ends.
Inputs may be any that keep to these rules, and one draw needn't show every extreme that they name: `face_link`: Symmetric: a subdomain has a face toward a neighbour exactly when that neighbour has the face back; no face points out of the grid; some subdomain has all four faces. `face_start`: the four entries of a subdomain are 512 times a permutation of 0, 1, 2, 3. Symmetric blocks; each subdomain's whole panel matrix, with schur_diag on the block diagonal and coupling and its transpose beside it, is positive definite.
All inputs are finite; a program needn't handle non-finite values.
Results may differ from the reference program's by a relative error of at most 0.0004.
Values may be sent and summed in bfloat16 or wider, within the bound.
A program may use at most 64 MiB of HBM per device.

```python
import math
import jax
import jax.numpy as jnp
from jax import lax

F = 512
SLOTS = 4
ITERS = 2
SUB_X = 8
SUB_Y = 4


def drawn_scales(key):
    lowest = math.log(0.5)
    return jnp.exp(jax.random.uniform(jax.random.fold_in(key, 11), (SUB_Y, SUB_X, SLOTS, F), jnp.float32, lowest, -lowest))


def pick_scales(key):
    return drawn_scales(key)


def kernel_parts(key):
    ratio = jax.random.uniform(jax.random.fold_in(key, 21), (SUB_Y, SUB_X, 1, 1, 1), jnp.float32, 0.8, 0.92)
    rate = -jnp.log(ratio)
    lowest = math.log(0.5)
    amplitude = jnp.exp(jax.random.uniform(jax.random.fold_in(key, 22), (SUB_Y, SUB_X, 1, 1, 1), jnp.float32, lowest, -lowest))
    index = jnp.arange(F, dtype=jnp.float32)
    distance = jnp.abs(index[:, None] - index[None, :])
    kernel = amplitude * jnp.exp(-rate * distance)
    spread = 0.3 * (1.0 - ratio) / ((1.0 + ratio) * amplitude)
    return (kernel, spread)


def rough_part(key, count, symmetric):
    marker = 31 if symmetric else 32
    noise = jax.random.uniform(jax.random.fold_in(key, marker), (SUB_Y, SUB_X, count, F, F), jnp.float32, -1.0, 1.0)
    if symmetric:
        noise = 0.5 * (noise + jnp.swapaxes(noise, -1, -2))
    return noise


def draw_schur_diag(key, part):
    scales = pick_scales(key)
    kernel, spread = kernel_parts(key)
    lifted = jax.random.uniform(jax.random.fold_in(key, 2), (SUB_Y, SUB_X, SLOTS, F, 1), jnp.float32, 1.0, 2.0)
    diagonal = jnp.arange(F)[:, None] == jnp.arange(F)[None, :]
    unscaled = jnp.where(diagonal, lifted, 0.0) + kernel * (1.0 + spread * rough_part(key, SLOTS, True))
    return (unscaled * scales[..., :, None] * scales[..., None, :]).astype(jnp.bfloat16)


def draw_coupling(key, part):
    scales = pick_scales(key)
    kernel, spread = kernel_parts(key)
    weight = jax.random.uniform(jax.random.fold_in(key, 23), (SUB_Y, SUB_X, SLOTS - 1, 1, 1), jnp.float32, 0.2, 0.45)
    unscaled = kernel * (weight + spread * rough_part(key, SLOTS - 1, False))
    return (unscaled * scales[..., :-1, :, None] * scales[..., 1:, None, :]).astype(jnp.bfloat16)


def draw_right_side(key, part):
    column = jnp.arange(SUB_X, dtype=jnp.float32)
    ramp = (1.0 + 2.0 * column / (SUB_X - 1))[None, :, None, None]
    values = jnp.clip(jax.random.normal(key, (SUB_Y, SUB_X, SLOTS, F), jnp.float32), -4.0, 4.0)
    return values * ramp


def draw_face_start(key, part):
    scores = jax.random.randint(key, (SUB_Y, SUB_X, SLOTS), 0, 1048576) * SLOTS + jnp.arange(SLOTS, dtype=jnp.int32)
    order = jnp.argsort(scores, axis=-1, stable=True).astype(jnp.int32)
    return order * F


def draw_face_link(key, part):
    across = jax.random.randint(jax.random.fold_in(key, 1), (SUB_Y, SUB_X - 1), 0, 10) < 7
    vertical = jax.random.randint(jax.random.fold_in(key, 2), (SUB_Y - 1, SUB_X), 0, 10) < 7
    center_y = jax.random.randint(jax.random.fold_in(key, 3), (), 1, SUB_Y - 1)
    center_x = jax.random.randint(jax.random.fold_in(key, 4), (), 1, SUB_X - 1)
    rows_a = jnp.arange(SUB_Y)[:, None]
    cols_a = jnp.arange(SUB_X - 1)[None, :]
    across = across | (rows_a == center_y) & ((cols_a == center_x - 1) | (cols_a == center_x))
    rows_v = jnp.arange(SUB_Y - 1)[:, None]
    cols_v = jnp.arange(SUB_X)[None, :]
    vertical = vertical | (cols_v == center_x) & ((rows_v == center_y - 1) | (rows_v == center_y))
    across = across.astype(jnp.int32)
    vertical = vertical.astype(jnp.int32)
    western = jnp.pad(across, ((0, 0), (1, 0)))
    eastern = jnp.pad(across, ((0, 0), (0, 1)))
    southern = jnp.pad(vertical, ((1, 0), (0, 0)))
    northern = jnp.pad(vertical, ((0, 1), (0, 0)))
    return jnp.stack([western, eastern, southern, northern], axis=-1).astype(jnp.int32)


def setup_inputs(seed: int = 0) -> dict:
    splits = jax.random.split(jax.random.key(seed), 6)
    schur_diag = draw_schur_diag(jax.random.fold_in(splits[5], 71), 0)
    coupling = draw_coupling(jax.random.fold_in(splits[5], 71), 0)
    right_side = draw_right_side(jax.random.fold_in(splits[5], 71), 0)
    face_link = draw_face_link(jax.random.fold_in(splits[5], 71), 0)
    face_start = draw_face_start(jax.random.fold_in(splits[5], 71), 0)
    return dict(schur_diag=schur_diag, coupling=coupling, right_side=right_side, face_link=face_link, face_start=face_start)


highest = lax.Precision.HIGHEST

def inverse_slots(slot_ids):
    numbers = jnp.arange(SLOTS, dtype=jnp.int32)
    matched = slot_ids[..., :, None] == numbers
    return jnp.sum(jnp.where(matched, numbers[:, None], 0), axis=-2).astype(jnp.int32)

def to_panel(values, slot_ids):
    return jnp.take_along_axis(values, inverse_slots(slot_ids)[..., None], axis=-2)

def to_faces(values, slot_ids):
    return jnp.take_along_axis(values, slot_ids[..., None], axis=-2)

def panel_terms(blocks, coupling, vectors, with_diag):
    linked = coupling.astype(jnp.float32)
    upward = jnp.einsum('...pij,...pj->...pi', linked, vectors[..., 1:, :], precision=highest)
    downward = jnp.einsum('...pji,...pj->...pi', linked, vectors[..., :-1, :], precision=highest)
    border = jnp.zeros_like(vectors[..., :1, :])
    totals = jnp.concatenate([upward, border], axis=-2) + jnp.concatenate([border, downward], axis=-2)
    if with_diag:
        totals = jnp.einsum('...pij,...pj->...pi', blocks.astype(jnp.float32), vectors, precision=highest) + totals
    return totals

def solve_factor(factors, vectors):
    middle = jax.scipy.linalg.solve_triangular(factors, vectors[..., None], lower=True)
    return jax.scipy.linalg.solve_triangular(factors, middle, lower=True, trans=1)[..., 0]

def facing(values):
    column = jnp.zeros_like(values[:, :1, 0])
    western = jnp.concatenate([column, values[:, :-1, 1]], axis=1)
    eastern = jnp.concatenate([values[:, 1:, 0], column], axis=1)
    row_zero = jnp.zeros_like(values[:1, :, 0])
    southern = jnp.concatenate([row_zero, values[:-1, :, 3]], axis=0)
    northern = jnp.concatenate([values[1:, :, 2], row_zero], axis=0)
    return jnp.stack([western, eastern, southern, northern], axis=2)

def block_row(schur_diag, slot_ids, live_mask, row_index):

    def own_row(index):
        clipped = jnp.clip(index, 0, SUB_Y - 1).astype(jnp.int32)
        blocks = lax.dynamic_index_in_dim(schur_diag, clipped, 0, keepdims=False)
        chosen = lax.dynamic_index_in_dim(slot_ids, clipped, 0, keepdims=False)
        return jnp.take_along_axis(blocks, chosen[:, :, None, None], axis=1)
    center = own_row(row_index)
    below = own_row(row_index - 1)
    above = own_row(row_index + 1)
    single = jnp.zeros_like(center[:1, 0])
    partner = jnp.stack([jnp.concatenate([single, center[:-1, 1]], axis=0), jnp.concatenate([center[1:, 0], single], axis=0), below[:, 3], above[:, 2]], axis=1)
    summed = center.astype(jnp.float32) + partner.astype(jnp.float32)
    alive_row = lax.dynamic_index_in_dim(live_mask, row_index, 0, keepdims=False)
    identity = jnp.eye(F, dtype=jnp.float32)
    return jnp.where(alive_row[:, :, None, None], summed, identity)

def reference(schur_diag, coupling, right_side, face_link, face_start):
    slot_ids = (face_start // F).astype(jnp.int32)
    live_mask = face_link > 0
    alive = live_mask[..., None]
    row_ids = jnp.arange(SUB_Y, dtype=jnp.int32)
    factors = lax.map(lambda row_index: jnp.linalg.cholesky(block_row(schur_diag, slot_ids, live_mask, row_index)), row_ids)

    def assemble(values):
        return jnp.where(alive, values + facing(values), 0.0)

    def local_term(values, with_diag):
        panel = to_panel(jnp.where(alive, values, 0.0), slot_ids)
        terms = lax.map(lambda members: panel_terms(members[0], members[1], members[2], with_diag), (schur_diag, coupling, panel))
        return jnp.where(alive, to_faces(terms, slot_ids), 0.0)

    def apply_operator(values):
        return assemble(local_term(values, True))

    def precondition(values):
        first_solve = solve_factor(factors, values)
        spread = assemble(local_term(first_solve, False))
        return jnp.where(alive, solve_factor(factors, values - spread), 0.0)

    def inner(first_vec, second_vec):
        return 0.5 * jnp.sum(first_vec * second_vec)
    residual = assemble(right_side)
    solution = jnp.zeros_like(residual)
    precond_res = precondition(residual)
    direction = precond_res
    current = inner(residual, precond_res)
    for iteration in range(ITERS):
        image = apply_operator(direction)
        alpha_step = current / inner(direction, image)
        solution = solution + alpha_step * direction
        residual = residual - alpha_step * image
        if iteration + 1 < ITERS:
            precond_res = precondition(residual)
            following = inner(residual, precond_res)
            direction = precond_res + following / current * direction
            current = following
    return (solution, residual)
```

```python
import functools

import jax
import jax.numpy as jnp
from jax import lax
from jax.experimental import pallas as pl
from jax.experimental.pallas import tpu as pltpu
from jax.sharding import PartitionSpec as P

ITERS = 2
B = 128
G = 8
MESH = pl.DeviceIdType.MESH
f32 = jnp.float32
bf16 = jnp.bfloat16


def pieces(x):
    h = x.astype(bf16).astype(f32)
    x = x - h
    m = x.astype(bf16).astype(f32)
    return h, m, (x - m).astype(bf16).astype(f32)


LHS_ORDER = (0, 0, 1, 1, 0, 2)
RHS_ORDER = (0, 1, 0, 1, 2, 0)


def stacked(x, order, axis):
    parts = pieces(x)
    return jnp.concatenate([parts[i] for i in order], axis=axis).astype(bf16)


def contract(lhs, rhs, lhs_dim, rhs_dim):
    return lax.dot_general(
        lhs, rhs, (((lhs_dim,), (rhs_dim,)), ((), ())), preferred_element_type=f32
    )


def leaf_sweep(d_ref):
    faces = d_ref.shape[0]
    lane = lax.broadcasted_iota(jnp.int32, (faces, G, B), 2)
    sub = lax.broadcasted_iota(jnp.int32, (faces, G, B), 1)
    wide = lax.broadcasted_iota(jnp.int32, (B, B), 1)

    def group(g, carry):
        base = pl.multiple_of(g * G, G)
        rows = d_ref[:, pl.ds(base, G), :]
        back = lax.rem(B - base, B)
        w = jnp.stack([pltpu.roll(rows[f], back, 1) for f in range(faces)])
        for j in range(G):
            col = w[:, :, j : j + 1]
            row = w[:, j : j + 1, :]
            inv = 1.0 / w[:, j : j + 1, j : j + 1]
            here = lane == j
            r = jnp.where(here[:, :1], 1.0, row) * inv
            w = jnp.where(sub == j, r, jnp.where(here, 0.0, w) - col * r)
        w = jnp.where(lane < G, -w, w)
        w = [pltpu.roll(w[f], base, 1) for f in range(faces)]
        mine = (wide >= base) & (wide < base + G)
        for f in range(faces):
            left = stacked(rows[f], LHS_ORDER, 0)
            right = stacked(w[f], RHS_ORDER, 0)
            d_ref[f] = jnp.where(mine, 0.0, d_ref[f]) - contract(left, right, 0, 0)
        for f in range(faces):
            d_ref[f, pl.ds(base, G), :] = w[f]
        return carry

    lax.fori_loop(0, B // G, group, 0)


def invert_kernel(live_ref, *refs):
    inv_ref, a_ref, d_ref = refs[-3:]
    faces, n, _ = a_ref.shape
    own, part = refs[:faces], refs[faces : 2 * faces]
    for f in range(faces):
        eye = (
            lax.broadcasted_iota(jnp.int32, (n, n), 0)
            == lax.broadcasted_iota(jnp.int32, (n, n), 1)
        ).astype(f32)
        summed = own[f][...].astype(f32) + part[f][...].astype(f32)
        summed = 0.5 * (summed + summed.T)
        a_ref[f] = jnp.where(live_ref[f] > 0, summed, eye)

    def stage(s, carry):
        base = pl.multiple_of(s * B, B)
        d_ref[...] = a_ref[:, pl.ds(base, B), pl.ds(base, B)]
        leaf_sweep(d_ref)

        def face(f, carry):
            neg = d_ref[f]
            rows = a_ref[f, pl.ds(base, B), :]
            cols = a_ref[f, :, pl.ds(base, B)]
            w = -contract(
                stacked(neg, LHS_ORDER, 1), stacked(rows, RHS_ORDER, 0), 1, 0
            )
            a_ref[f, pl.ds(base, B), :] = w
            a_ref[f, pl.ds(base, B), pl.ds(base, B)] = neg
            w = a_ref[f, pl.ds(base, B), :]
            left = stacked(cols, LHS_ORDER, 1)
            right = stacked(w, RHS_ORDER, 0)
            half = n // 2
            for h in range(2):
                lane = lax.broadcasted_iota(jnp.int32, (n, half), 1) + h * half
                mine = (lane >= base) & (lane < base + B)
                old = a_ref[f, :, h * half : (h + 1) * half]
                a_ref[f, :, h * half : (h + 1) * half] = jnp.where(
                    mine, 0.0, old
                ) - contract(left, right[:, h * half : (h + 1) * half], 1, 0)
            a_ref[f, pl.ds(base, B), :] = w
            return carry

        lax.fori_loop(0, faces, face, 0)
        return carry

    lax.fori_loop(0, n // B, stage, 0)
    for f in range(faces):
        for i, piece in enumerate(pieces(-a_ref[f])):
            inv_ref[i, f] = piece.astype(bf16)


def cg_kernel(
    nx, ny, live_ref, slot_ref, rhs_ref, inv_ref, diag_ref, coup_ref,
    sol_ref, res_ref,
    send_buf, recv_buf, xbuf, ybuf, vs_sem, vr_sem, xs_sem, xr_sem, ys_sem, yr_sem,
):
    mx, my = lax.axis_index("sx"), lax.axis_index("sy")
    faces, n = rhs_ref.shape
    recv_buf[...] = jnp.zeros_like(recv_buf)
    send_buf[...] = jnp.zeros_like(send_buf)

    barrier = pltpu.get_barrier_semaphore()
    for o in range(1, nx):
        pl.semaphore_signal(
            barrier, inc=1, device_id={"sx": lax.rem(mx + o, nx), "sy": my}, device_id_type=MESH
        )
    for o in range(1, ny):
        pl.semaphore_signal(
            barrier, inc=1, device_id={"sx": mx, "sy": lax.rem(my + o, ny)}, device_id_type=MESH
        )
    pl.semaphore_wait(barrier, nx + ny - 2)

    sub = lax.broadcasted_iota(jnp.int32, (8, n), 0)
    alive = jnp.zeros((8, n), jnp.bool_)
    slots = jnp.full((8, n), -1, jnp.int32)
    for d in range(faces):
        alive = alive | ((sub == d) & (live_ref[d] > 0))
        slots = jnp.where(sub == d, slot_ref[d], slots)

    guards = (mx > 0, mx < nx - 1, my > 0, my < ny - 1)
    targets = (
        {"sx": mx - 1, "sy": my},
        {"sx": mx + 1, "sy": my},
        {"sx": mx, "sy": my - 1},
        {"sx": mx, "sy": my + 1},
    )

    def vector_copy(phase, d):
        return pltpu.make_async_remote_copy(
            src_ref=send_buf.at[phase, d],
            dst_ref=recv_buf.at[phase, d ^ 1],
            send_sem=vs_sem.at[phase, d],
            recv_sem=vr_sem.at[phase, d ^ 1],
            device_id=targets[d],
            device_id_type=MESH,
        )

    def swap_start(phase, field):
        for d in range(faces):
            send_buf[phase, d, 0:1, :] = field[d : d + 1]

            @pl.when(guards[d])
            def _():
                vector_copy(phase, d).start()

    def swap_finish(phase, field):
        for d in range(faces):

            @pl.when(guards[d])
            def _():
                vector_copy(phase, d).wait_send()
                pltpu.make_async_remote_copy(
                    src_ref=send_buf.at[phase, d ^ 1],
                    dst_ref=recv_buf.at[phase, d],
                    send_sem=vs_sem.at[phase, d ^ 1],
                    recv_sem=vr_sem.at[phase, d],
                    device_id=targets[d],
                    device_id_type=MESH,
                ).wait_recv()

        for d in range(faces):
            field = jnp.where(sub == d, field + recv_buf[phase, d, 0:1, :], field)
        return jnp.where(alive, field, 0.0)

    def ring_copy(buf, send, recv, phase, me, peer, o, device):
        return pltpu.make_async_remote_copy(
            src_ref=buf.at[phase, me],
            dst_ref=buf.at[phase, me],
            send_sem=send.at[phase, o],
            recv_sem=recv.at[phase, me],
            device_id=device,
            device_id_type=MESH,
        )

    def gather_all(buf, send, recv, phase, tile, size, me, device):
        buf[phase, me] = tile
        for o in range(1, size):
            peer = lax.rem(me + o, size)
            ring_copy(buf, send, recv, phase, me, peer, o, device(peer)).start()

    def gather_end(buf, send, recv, phase, size, me, device):
        for o in range(1, size):
            peer = lax.rem(me + o, size)
            ring_copy(buf, send, recv, phase, me, peer, o, device(peer)).wait_send()
            pltpu.make_async_remote_copy(
                src_ref=buf.at[phase, peer],
                dst_ref=buf.at[phase, peer],
                send_sem=send.at[phase, o],
                recv_sem=recv.at[phase, peer],
                device_id=device(peer),
                device_id_type=MESH,
            ).wait_recv()
        return jnp.sum(buf[phase], axis=0)

    def reduce_start(phase, products):
        tile = jnp.zeros((8, B), f32)
        row = lax.broadcasted_iota(jnp.int32, (8, B), 0)
        for q, prod in enumerate(products):
            part = sum(prod[:, i * B : (i + 1) * B] for i in range(n // B))
            tile = jnp.where(row == q, jnp.sum(part, axis=0, keepdims=True), tile)
        gather_all(
            xbuf, xs_sem, xr_sem, phase, tile, nx, mx, lambda p: {"sx": p, "sy": my}
        )

    def reduce_finish(phase, count):
        tile = gather_end(xbuf, xs_sem, xr_sem, phase, nx, mx, lambda p: {"sx": p, "sy": my})
        gather_all(ybuf, ys_sem, yr_sem, phase, tile, ny, my, lambda p: {"sx": mx, "sy": p})
        tile = gather_end(ybuf, ys_sem, yr_sem, phase, ny, my, lambda p: {"sx": mx, "sy": p})
        total = jnp.sum(tile, axis=1, keepdims=True)
        return [total[q : q + 1] for q in range(count)]

    def lifted(field):
        return jnp.concatenate(pieces(field), axis=0).astype(bf16)

    def gathered(out):
        return out[0:8] + out[8:16] + out[16:24]

    def per_face(left, matrices):
        total = jnp.zeros((8, n), f32)
        for d in range(faces):
            out = sum(gathered(contract(left, m, 1, 0)) for m in matrices(d))
            total = jnp.where(sub == d, out, total)
        return total

    def apply_inverse(field):
        return per_face(lifted(field), lambda d: [inv_ref[i, d] for i in range(3)])

    def local_term(field, with_diag):
        field = jnp.where(alive, field, 0.0)
        panel = jnp.zeros((8, n), f32)
        for d in range(faces):
            panel = jnp.where(sub == slot_ref[d], field[d : d + 1], panel)
        left = lifted(panel)
        terms = jnp.zeros((8, n), f32)
        for p in range(faces - 1):
            up = gathered(contract(left, coup_ref[p], 1, 1))
            down = gathered(contract(left, coup_ref[p], 1, 0))
            terms = terms + jnp.where(sub == p, up[p + 1 : p + 2], 0.0)
            terms = terms + jnp.where(sub == p + 1, down[p : p + 1], 0.0)
        if with_diag:
            for p in range(faces):
                out = gathered(contract(left, diag_ref[p], 1, 1))
                terms = terms + jnp.where(sub == p, out, 0.0)
        back = jnp.zeros((8, n), f32)
        for p in range(faces):
            back = jnp.where(slots == p, terms[p : p + 1], back)
        return jnp.where(alive, back, 0.0)

    def precondition(phase, field):
        first = apply_inverse(field)
        spread = local_term(first, False)
        swap_start(phase, spread)
        spread = swap_finish(phase, spread)
        return jnp.where(alive, apply_inverse(field - spread), 0.0)

    source = jnp.concatenate([rhs_ref[...], jnp.zeros((8 - faces, n), f32)], axis=0)
    swap_start(0, source)
    residual = swap_finish(0, source)
    solution = jnp.zeros_like(residual)
    for it in range(ITERS):
        z = precondition(1 + 2 * it, residual)
        term = local_term(z, True)
        swap_start(2 + 2 * it, term)
        products = [0.5 * residual * z, z * term]
        if it:
            products += [z * term_sum + direction * term]
        reduce_start(it, products)
        sums = reduce_finish(it, len(products))
        image_z = swap_finish(2 + 2 * it, term)
        if it == 0:
            rho, curve = sums
            direction, image, term_sum = z, image_z, term
        else:
            new, own, cross = sums
            beta = new / rho
            curve = own + beta * (cross + beta * curve)
            direction = z + beta * direction
            image = image_z + beta * image
            term_sum = term + beta * term_sum
            rho = new
        alpha = rho / curve
        solution = solution + alpha * direction
        residual = residual - alpha * image
    sol_ref[...] = solution[0:faces]
    res_ref[...] = residual[0:faces]


def trade_blocks(blocks):
    nx, ny = lax.axis_size("sx"), lax.axis_size("sy")
    right = [(i, i + 1) for i in range(nx - 1)]
    upper = [(i, i + 1) for i in range(ny - 1)]
    west = lax.ppermute(blocks[1], "sx", right)
    east = lax.ppermute(blocks[0], "sx", [(j, i) for i, j in right])
    south = lax.ppermute(blocks[3], "sy", upper)
    north = lax.ppermute(blocks[2], "sy", [(j, i) for i, j in upper])
    return west, east, south, north


def body(nx, ny, schur_diag, coupling, right_side, face_link, face_start):
    blocks, linked, source = schur_diag[0, 0], coupling[0, 0], right_side[0, 0]
    faces, n, _ = blocks.shape
    live = face_link[0, 0]
    slots = face_start[0, 0] // n
    own = [lax.dynamic_index_in_dim(blocks, slots[d], 0, False) for d in range(faces)]
    partner = trade_blocks(own)
    vmem = pl.BlockSpec(memory_space=pltpu.VMEM)
    smem = pl.BlockSpec(memory_space=pltpu.SMEM)
    inverses = pl.pallas_call(
        invert_kernel,
        out_shape=jax.ShapeDtypeStruct((3, faces, n, n), bf16),
        in_specs=[smem] + [vmem] * (2 * faces),
        out_specs=vmem,
        scratch_shapes=[
            pltpu.VMEM((faces, n, n), f32),
            pltpu.VMEM((faces, B, B), f32),
        ],
        compiler_params=pltpu.CompilerParams(vmem_limit_bytes=48 * 2**20),
    )(live, *own, *partner)
    phases = 1 + 2 * ITERS
    sol, res = pl.pallas_call(
        functools.partial(cg_kernel, nx, ny),
        out_shape=[jax.ShapeDtypeStruct((faces, n), f32)] * 2,
        in_specs=[smem, smem] + [vmem] * 4,
        out_specs=[vmem, vmem],
        scratch_shapes=[
            pltpu.VMEM((phases, faces, 8, n), f32),
            pltpu.VMEM((phases, faces, 8, n), f32),
            pltpu.VMEM((ITERS, nx, 8, B), f32),
            pltpu.VMEM((ITERS, ny, 8, B), f32),
            pltpu.SemaphoreType.DMA((phases, faces)),
            pltpu.SemaphoreType.DMA((phases, faces)),
            pltpu.SemaphoreType.DMA((ITERS, nx)),
            pltpu.SemaphoreType.DMA((ITERS, nx)),
            pltpu.SemaphoreType.DMA((ITERS, ny)),
            pltpu.SemaphoreType.DMA((ITERS, ny)),
        ],
        compiler_params=pltpu.CompilerParams(
            collective_id=0, has_side_effects=True, vmem_limit_bytes=48 * 2**20
        ),
    )(live, slots, source, inverses, blocks, linked)
    return sol[None, None], res[None, None]


def solution(mesh):
    shape = dict(mesh.shape)
    return jax.shard_map(
        functools.partial(body, shape["sx"], shape["sy"]),
        mesh=mesh,
        in_specs=(
            P("sy", "sx", None, None, None),
            P("sy", "sx", None, None, None),
            P("sy", "sx", None, None),
            P("sy", "sx", None),
            P("sy", "sx", None),
        ),
        out_specs=(P("sy", "sx", None, None), P("sy", "sx", None, None)),
        check_vma=False,
    )
```

```python
import functools

import jax
import jax.numpy as jnp
from jax import lax
from jax.experimental import pallas as pl
from jax.experimental.pallas import tpu as pltpu
from jax.sharding import PartitionSpec as P

ITERS = 2
B = 128
G = 8
MESH = pl.DeviceIdType.MESH
f32 = jnp.float32
bf16 = jnp.bfloat16


def pieces(x):
    h = x.astype(bf16).astype(f32)
    x = x - h
    m = x.astype(bf16).astype(f32)
    return h, m, (x - m).astype(bf16).astype(f32)


LHS_ORDER = (0, 0, 1, 1, 0, 2)
RHS_ORDER = (0, 1, 0, 1, 2, 0)


def stacked(x, order, axis):
    parts = pieces(x)
    return jnp.concatenate([parts[i] for i in order], axis=axis).astype(bf16)


def contract(lhs, rhs, lhs_dim, rhs_dim):
    return lax.dot_general(
        lhs, rhs, (((lhs_dim,), (rhs_dim,)), ((), ())), preferred_element_type=f32
    )


def leaf_sweep(d_ref):
    faces = d_ref.shape[0]
    lane = lax.broadcasted_iota(jnp.int32, (faces, G, B), 2)
    sub = lax.broadcasted_iota(jnp.int32, (faces, G, B), 1)
    wide = lax.broadcasted_iota(jnp.int32, (B, B), 1)

    def group(g, carry):
        base = pl.multiple_of(g * G, G)
        rows = d_ref[:, pl.ds(base, G), :]
        back = lax.rem(B - base, B)
        w = jnp.stack([pltpu.roll(rows[f], back, 1) for f in range(faces)])
        for j in range(G):
            col = jnp.broadcast_to(w[:, :, j : j + 1], w.shape)
            row = w[:, j : j + 1, :]
            inv = pl.reciprocal(col[:, j : j + 1, :], approx=False)
            here = lane == j
            r = jnp.where(here[:, :1], 1.0, row) * inv
            w = jnp.where(sub == j, r, jnp.where(here, 0.0, w) - col * r)
        w = jnp.where(lane < G, -w, w)
        w = [pltpu.roll(w[f], base, 1) for f in range(faces)]
        mine = (wide >= base) & (wide < base + G)
        for f in range(faces):
            left = stacked(rows[f], LHS_ORDER, 0)
            right = stacked(w[f], RHS_ORDER, 0)
            d_ref[f] = jnp.where(mine, 0.0, d_ref[f]) - contract(left, right, 0, 0)
        for f in range(faces):
            d_ref[f, pl.ds(base, G), :] = w[f]
        return carry

    lax.fori_loop(0, B // G, group, 0)


def invert_kernel(live_ref, *refs):
    inv_ref, a_ref, d_ref = refs[-3:]
    faces, n, _ = a_ref.shape
    own, part = refs[:faces], refs[faces : 2 * faces]
    for f in range(faces):
        eye = (
            lax.broadcasted_iota(jnp.int32, (n, n), 0)
            == lax.broadcasted_iota(jnp.int32, (n, n), 1)
        ).astype(f32)
        summed = own[f][...].astype(f32) + part[f][...].astype(f32)
        summed = 0.5 * (summed + summed.T)
        a_ref[f] = jnp.where(live_ref[f] > 0, summed, eye)

    def stage(s, carry):
        base = pl.multiple_of(s * B, B)
        d_ref[...] = a_ref[:, pl.ds(base, B), pl.ds(base, B)]
        leaf_sweep(d_ref)

        def face(f, carry):
            neg = d_ref[f]
            rows = a_ref[f, pl.ds(base, B), :]
            cols = a_ref[f, :, pl.ds(base, B)]
            w = -contract(
                stacked(neg, LHS_ORDER, 1), stacked(rows, RHS_ORDER, 0), 1, 0
            )
            a_ref[f, pl.ds(base, B), :] = w
            a_ref[f, pl.ds(base, B), pl.ds(base, B)] = neg
            w = a_ref[f, pl.ds(base, B), :]
            left = stacked(cols, LHS_ORDER, 1)
            right = stacked(w, RHS_ORDER, 0)
            half = n // 2
            for h in range(2):
                lane = lax.broadcasted_iota(jnp.int32, (n, half), 1) + h * half
                mine = (lane >= base) & (lane < base + B)
                old = a_ref[f, :, h * half : (h + 1) * half]
                a_ref[f, :, h * half : (h + 1) * half] = jnp.where(
                    mine, 0.0, old
                ) - contract(left, right[:, h * half : (h + 1) * half], 1, 0)
            a_ref[f, pl.ds(base, B), :] = w
            return carry

        lax.fori_loop(0, faces, face, 0)
        return carry

    lax.fori_loop(0, n // B, stage, 0)
    for f in range(faces):
        for i, piece in enumerate(pieces(-a_ref[f])):
            inv_ref[i, f] = piece.astype(bf16)


def cg_kernel(
    nx, ny, live_ref, slot_ref, rhs_ref, inv_ref, diag_ref, coup_ref,
    sol_ref, res_ref,
    send_buf, recv_buf, xbuf, ybuf, vs_sem, vr_sem, xs_sem, xr_sem, ys_sem, yr_sem,
):
    mx, my = lax.axis_index("sx"), lax.axis_index("sy")
    faces, n = rhs_ref.shape
    recv_buf[...] = jnp.zeros_like(recv_buf)
    send_buf[...] = jnp.zeros_like(send_buf)

    barrier = pltpu.get_barrier_semaphore()
    for o in range(1, nx):
        pl.semaphore_signal(
            barrier, inc=1, device_id={"sx": lax.rem(mx + o, nx), "sy": my}, device_id_type=MESH
        )
    for o in range(1, ny):
        pl.semaphore_signal(
            barrier, inc=1, device_id={"sx": mx, "sy": lax.rem(my + o, ny)}, device_id_type=MESH
        )
    pl.semaphore_wait(barrier, nx + ny - 2)

    sub = lax.broadcasted_iota(jnp.int32, (8, n), 0)
    alive = jnp.zeros((8, n), jnp.bool_)
    slots = jnp.full((8, n), -1, jnp.int32)
    for d in range(faces):
        alive = alive | ((sub == d) & (live_ref[d] > 0))
        slots = jnp.where(sub == d, slot_ref[d], slots)

    guards = (mx > 0, mx < nx - 1, my > 0, my < ny - 1)
    targets = (
        {"sx": mx - 1, "sy": my},
        {"sx": mx + 1, "sy": my},
        {"sx": mx, "sy": my - 1},
        {"sx": mx, "sy": my + 1},
    )

    def vector_copy(phase, d):
        return pltpu.make_async_remote_copy(
            src_ref=send_buf.at[phase, d],
            dst_ref=recv_buf.at[phase, d ^ 1],
            send_sem=vs_sem.at[phase, d],
            recv_sem=vr_sem.at[phase, d ^ 1],
            device_id=targets[d],
            device_id_type=MESH,
        )

    def swap_start(phase, field):
        for d in range(faces):
            send_buf[phase, d, 0:1, :] = field[d : d + 1]

            @pl.when(guards[d])
            def _():
                vector_copy(phase, d).start()

    def swap_finish(phase, field):
        for d in range(faces):

            @pl.when(guards[d])
            def _():
                vector_copy(phase, d).wait_send()
                pltpu.make_async_remote_copy(
                    src_ref=send_buf.at[phase, d ^ 1],
                    dst_ref=recv_buf.at[phase, d],
                    send_sem=vs_sem.at[phase, d ^ 1],
                    recv_sem=vr_sem.at[phase, d],
                    device_id=targets[d],
                    device_id_type=MESH,
                ).wait_recv()

        for d in range(faces):
            field = jnp.where(sub == d, field + recv_buf[phase, d, 0:1, :], field)
        return jnp.where(alive, field, 0.0)

    def ring_copy(buf, send, recv, phase, me, peer, o, device):
        return pltpu.make_async_remote_copy(
            src_ref=buf.at[phase, me],
            dst_ref=buf.at[phase, me],
            send_sem=send.at[phase, o],
            recv_sem=recv.at[phase, me],
            device_id=device,
            device_id_type=MESH,
        )

    def gather_all(buf, send, recv, phase, tile, size, me, device):
        buf[phase, me] = tile
        for o in range(1, size):
            peer = lax.rem(me + o, size)
            ring_copy(buf, send, recv, phase, me, peer, o, device(peer)).start()

    def gather_end(buf, send, recv, phase, size, me, device):
        for o in range(1, size):
            peer = lax.rem(me + o, size)
            ring_copy(buf, send, recv, phase, me, peer, o, device(peer)).wait_send()
            pltpu.make_async_remote_copy(
                src_ref=buf.at[phase, peer],
                dst_ref=buf.at[phase, peer],
                send_sem=send.at[phase, o],
                recv_sem=recv.at[phase, peer],
                device_id=device(peer),
                device_id_type=MESH,
            ).wait_recv()
        return jnp.sum(buf[phase], axis=0)

    def reduce_start(phase, products):
        tile = jnp.zeros((8, B), f32)
        row = lax.broadcasted_iota(jnp.int32, (8, B), 0)
        for q, prod in enumerate(products):
            part = sum(prod[:, i * B : (i + 1) * B] for i in range(n // B))
            tile = jnp.where(row == q, jnp.sum(part, axis=0, keepdims=True), tile)
        gather_all(
            xbuf, xs_sem, xr_sem, phase, tile, nx, mx, lambda p: {"sx": p, "sy": my}
        )

    def reduce_finish(phase, count):
        tile = gather_end(xbuf, xs_sem, xr_sem, phase, nx, mx, lambda p: {"sx": p, "sy": my})
        gather_all(ybuf, ys_sem, yr_sem, phase, tile, ny, my, lambda p: {"sx": mx, "sy": p})
        tile = gather_end(ybuf, ys_sem, yr_sem, phase, ny, my, lambda p: {"sx": mx, "sy": p})
        total = jnp.sum(tile, axis=1, keepdims=True)
        return [total[q : q + 1] for q in range(count)]

    def lifted(field):
        return jnp.concatenate(pieces(field), axis=0).astype(bf16)

    def gathered(out):
        return out[0:8] + out[8:16] + out[16:24]

    def per_face(left, matrices):
        total = jnp.zeros((8, n), f32)
        for d in range(faces):
            out = sum(gathered(contract(left, m, 1, 0)) for m in matrices(d))
            total = jnp.where(sub == d, out, total)
        return total

    def apply_inverse(field):
        return per_face(lifted(field), lambda d: [inv_ref[i, d] for i in range(3)])

    def local_term(field, with_diag):
        field = jnp.where(alive, field, 0.0)
        panel = jnp.zeros((8, n), f32)
        for d in range(faces):
            panel = jnp.where(sub == slot_ref[d], field[d : d + 1], panel)
        left = lifted(panel)
        terms = jnp.zeros((8, n), f32)
        for p in range(faces - 1):
            up = gathered(contract(left, coup_ref[p], 1, 1))
            down = gathered(contract(left, coup_ref[p], 1, 0))
            terms = terms + jnp.where(sub == p, up[p + 1 : p + 2], 0.0)
            terms = terms + jnp.where(sub == p + 1, down[p : p + 1], 0.0)
        if with_diag:
            for p in range(faces):
                out = gathered(contract(left, diag_ref[p], 1, 1))
                terms = terms + jnp.where(sub == p, out, 0.0)
        back = jnp.zeros((8, n), f32)
        for p in range(faces):
            back = jnp.where(slots == p, terms[p : p + 1], back)
        return jnp.where(alive, back, 0.0)

    def precondition(phase, field):
        first = apply_inverse(field)
        spread = local_term(first, False)
        swap_start(phase, spread)
        spread = swap_finish(phase, spread)
        return jnp.where(alive, apply_inverse(field - spread), 0.0)

    source = jnp.concatenate([rhs_ref[...], jnp.zeros((8 - faces, n), f32)], axis=0)
    swap_start(0, source)
    residual = swap_finish(0, source)
    solution = jnp.zeros_like(residual)
    for it in range(ITERS):
        z = precondition(1 + 2 * it, residual)
        term = local_term(z, True)
        swap_start(2 + 2 * it, term)
        products = [0.5 * residual * z, z * term]
        if it:
            products += [z * term_sum + direction * term]
        reduce_start(it, products)
        sums = reduce_finish(it, len(products))
        image_z = swap_finish(2 + 2 * it, term)
        if it == 0:
            rho, curve = sums
            direction, image, term_sum = z, image_z, term
        else:
            new, own, cross = sums
            beta = new / rho
            curve = own + beta * (cross + beta * curve)
            direction = z + beta * direction
            image = image_z + beta * image
            term_sum = term + beta * term_sum
            rho = new
        alpha = rho / curve
        solution = solution + alpha * direction
        residual = residual - alpha * image
    sol_ref[...] = solution[0:faces]
    res_ref[...] = residual[0:faces]


def trade_blocks(blocks):
    nx, ny = lax.axis_size("sx"), lax.axis_size("sy")
    right = [(i, i + 1) for i in range(nx - 1)]
    upper = [(i, i + 1) for i in range(ny - 1)]
    west = lax.ppermute(blocks[1], "sx", right)
    east = lax.ppermute(blocks[0], "sx", [(j, i) for i, j in right])
    south = lax.ppermute(blocks[3], "sy", upper)
    north = lax.ppermute(blocks[2], "sy", [(j, i) for i, j in upper])
    return west, east, south, north


def body(nx, ny, schur_diag, coupling, right_side, face_link, face_start):
    blocks, linked, source = schur_diag[0, 0], coupling[0, 0], right_side[0, 0]
    faces, n, _ = blocks.shape
    live = face_link[0, 0]
    slots = face_start[0, 0] // n
    own = [lax.dynamic_index_in_dim(blocks, slots[d], 0, False) for d in range(faces)]
    partner = trade_blocks(own)
    vmem = pl.BlockSpec(memory_space=pltpu.VMEM)
    smem = pl.BlockSpec(memory_space=pltpu.SMEM)
    inverses = pl.pallas_call(
        invert_kernel,
        out_shape=jax.ShapeDtypeStruct((3, faces, n, n), bf16),
        in_specs=[smem] + [vmem] * (2 * faces),
        out_specs=vmem,
        scratch_shapes=[
            pltpu.VMEM((faces, n, n), f32),
            pltpu.VMEM((faces, B, B), f32),
        ],
        compiler_params=pltpu.CompilerParams(vmem_limit_bytes=48 * 2**20),
    )(live, *own, *partner)
    phases = 1 + 2 * ITERS
    sol, res = pl.pallas_call(
        functools.partial(cg_kernel, nx, ny),
        out_shape=[jax.ShapeDtypeStruct((faces, n), f32)] * 2,
        in_specs=[smem, smem] + [vmem] * 4,
        out_specs=[vmem, vmem],
        scratch_shapes=[
            pltpu.VMEM((phases, faces, 8, n), f32),
            pltpu.VMEM((phases, faces, 8, n), f32),
            pltpu.VMEM((ITERS, nx, 8, B), f32),
            pltpu.VMEM((ITERS, ny, 8, B), f32),
            pltpu.SemaphoreType.DMA((phases, faces)),
            pltpu.SemaphoreType.DMA((phases, faces)),
            pltpu.SemaphoreType.DMA((ITERS, nx)),
            pltpu.SemaphoreType.DMA((ITERS, nx)),
            pltpu.SemaphoreType.DMA((ITERS, ny)),
            pltpu.SemaphoreType.DMA((ITERS, ny)),
        ],
        compiler_params=pltpu.CompilerParams(
            collective_id=0, has_side_effects=True, vmem_limit_bytes=48 * 2**20
        ),
    )(live, slots, source, inverses, blocks, linked)
    return sol[None, None], res[None, None]


def solution(mesh):
    shape = dict(mesh.shape)
    return jax.shard_map(
        functools.partial(body, shape["sx"], shape["sy"]),
        mesh=mesh,
        in_specs=(
            P("sy", "sx", None, None, None),
            P("sy", "sx", None, None, None),
            P("sy", "sx", None, None),
            P("sy", "sx", None),
            P("sy", "sx", None),
        ),
        out_specs=(P("sy", "sx", None, None), P("sy", "sx", None, None)),
        check_vma=False,
    )
```
